512 devices in a mesh: seq: 128 (over x, z, core), head: 4 (over y).
Axes of the slice: x: 4, y: 4, z: 16, core: 2. Of those that a mesh axis runs over, the one named last changes fastest.
Arguments:
- query_rot: bfloat16 [16384, 2048], P('seq', 'head'), may hold values from -6 to 6
- key_rot: bfloat16 [16384, 2048], P('seq', 'head'), may hold values from -6 to 6
- value_rot: bfloat16 [16384, 2048], P('seq', 'head'), may hold values from -6 to 6
- grad_out: bfloat16 [16384, 2048], P(('seq', 'head')), may hold values from -6 to 6
Outputs:
- attn_out: bfloat16 [16384, 2048], P(('seq', 'head'))
- grad_query: bfloat16 [16384, 2048], P('seq', 'head')
- grad_key: bfloat16 [16384, 2048], P('seq', 'head')
- grad_value: bfloat16 [16384, 2048], P('seq', 'head')
The draws below stay inside these ranges and needn't reach their ends.
All inputs are finite; a program needn't handle non-finite values.
Results may differ from the reference program's by a relative error of at most 0.0058.
Values may be sent and summed in bfloat16 or wider, within the bound.
A program may use at most 192 MiB of HBM per device.

```python
import jax
import jax.numpy as jnp
from jax import lax

HEADS = 32
DH = 64
GROUP = 128
TOKENS = 16384


def shard_levels(key, dims, cuts, least, high):
    def one(axis_at, parts):
        heights = jax.random.uniform(jax.random.fold_in(jax.random.fold_in(key, 6), axis_at), (parts,), jnp.float32, least / len(cuts), high / len(cuts))
        return jnp.repeat(jnp.exp(heights), dims[axis_at] // parts).reshape((-1,) + (1,) * (len(dims) - axis_at - 1))

    level = one(*cuts[0])
    for cut in cuts[1:]:
        level = level * one(*cut)
    return level


def normal_values(own_key, shape, scale, reach, shards=(), kind=jnp.bfloat16):
    values = scale * jax.random.normal(own_key, shape, jnp.float32)
    if shards:
        values = values * shard_levels(own_key, shape, shards, -0.22, 0.18)
    return jnp.clip(values, -reach, reach).astype(kind)


def setup_inputs(seed: int = 0) -> dict:
    keys = jax.random.split(jax.random.key(seed), 5)
    query_rot = normal_values(keys[0], (TOKENS, HEADS * DH), 1.0, 6.0, ((0, 128), (1, 4)))
    key_rot = normal_values(keys[1], (TOKENS, HEADS * DH), 1.0, 6.0, ((0, 128), (1, 4)))
    value_rot = normal_values(keys[2], (TOKENS, HEADS * DH), 1.0, 6.0, ((0, 128), (1, 4)))
    grad_out = normal_values(keys[3], (TOKENS, HEADS * DH), 1.0, 6.0, ((0, 512),))
    return dict(query_rot=query_rot, key_rot=key_rot, value_rot=value_rot, grad_out=grad_out)


def to_blocks(matrix):
    return matrix.reshape(TOKENS // GROUP, GROUP, HEADS, DH)

def masked(causal, left, right):
    products = jnp.einsum('thd,shd->hts', left.astype(jnp.float32), right.astype(jnp.float32))
    return jnp.where(causal, products, 0.0).astype(jnp.bfloat16)

def reference(query_rot, key_rot, value_rot, grad_out):
    positions = jnp.arange(TOKENS).astype(jnp.float32)
    factor = 1.0 / jnp.sqrt(DH * (positions + 1.0))
    scaled_query = (query_rot.astype(jnp.float32) * factor[:, None]).astype(jnp.bfloat16)
    scaled_grad = (grad_out.astype(jnp.float32) * factor[:, None]).astype(jnp.bfloat16)
    causal = jnp.tril(jnp.ones((GROUP, GROUP), jnp.bool_))
    pieces = (to_blocks(query_rot), to_blocks(key_rot), to_blocks(value_rot), to_blocks(scaled_query), to_blocks(scaled_grad))

    def forward_step(kv_state, items):
        plain_q, key_blk, value_blk, scale_q, scale_g = items
        kv_round = lax.optimization_barrier(kv_state.astype(jnp.bfloat16)).astype(kv_state.dtype)
        scores = masked(causal, scale_q, key_blk).astype(kv_state.dtype)
        grad_scores = masked(causal, scale_g, value_blk).astype(kv_state.dtype)
        value_f = value_blk.astype(kv_state.dtype)
        key_f = key_blk.astype(kv_state.dtype)
        attended = jnp.einsum('hts,shd->thd', scores, value_f) + jnp.einsum('thd,hde->the', scale_q.astype(kv_state.dtype), kv_round)
        grad_query = jnp.einsum('hts,shd->thd', grad_scores, key_f) + jnp.einsum('the,hde->thd', scale_g.astype(kv_state.dtype), kv_round)
        updated = kv_state + jnp.einsum('shd,she->hde', key_f, value_f)
        return (updated, (attended.astype(jnp.bfloat16), grad_query.astype(jnp.bfloat16)))

    def backward_step(grad_state, items):
        plain_q, key_blk, value_blk, scale_q, scale_g = items
        grad_round = lax.optimization_barrier(grad_state.astype(jnp.bfloat16)).astype(grad_state.dtype)
        grad_scores = masked(causal, scale_g, value_blk).astype(grad_state.dtype)
        plain_scores = masked(causal, plain_q, key_blk).astype(grad_state.dtype)
        query_f = plain_q.astype(grad_state.dtype)
        grad_f = scale_g.astype(grad_state.dtype)
        grad_key = jnp.einsum('hts,thd->shd', grad_scores, query_f) + jnp.einsum('she,hde->shd', value_blk.astype(grad_state.dtype), grad_round)
        grad_value = jnp.einsum('hts,the->she', plain_scores, grad_f) + jnp.einsum('sha,hae->she', key_blk.astype(grad_state.dtype), grad_round)
        updated = grad_state + jnp.einsum('thd,the->hde', query_f, grad_f)
        return (updated, (grad_key.astype(jnp.bfloat16), grad_value.astype(jnp.bfloat16)))
    start_state = jnp.zeros((HEADS, DH, DH), jnp.float32)
    unused, (attn_out, grad_query) = lax.scan(forward_step, start_state, pieces)
    unused_back, (grad_key, grad_value) = lax.scan(backward_step, start_state, pieces, reverse=True)
    width = HEADS * DH
    return (attn_out.reshape(TOKENS, width), grad_query.reshape(TOKENS, width), grad_key.reshape(TOKENS, width), grad_value.reshape(TOKENS, width))
```

```python
import functools

import jax
import jax.numpy as jnp
from jax import lax
from jax.experimental import pallas as pl
from jax.experimental.pallas import tpu as pltpu
from jax.sharding import PartitionSpec as P

DH = 64
GROUP = 128
XS = 4
ZS = 16
CORES = 2
PAIR = 2 * DH
HALF = DH // CORES
MESH = pl.DeviceIdType.MESH
F32 = jnp.float32
BF16 = jnp.bfloat16

NN = (((1,), (0,)), ((), ()))
NT = (((1,), (1,)), ((), ()))
TN = (((0,), (0,)), ((), ()))


def dot(a, b, dims=NN):
    return lax.dot_general(a, b, dims, preferred_element_type=F32)


def iota(shape, dim):
    return lax.broadcasted_iota(jnp.int32, shape, dim)


def kernel(
    xs, zs, ys,
    q_hbm, k_hbm, v_hbm, g_hbm,
    attn_o, gq_o, gk_o, gv_o,
    q, k, v, g,
    state_f, state_r,
    part_f, part_r,
    chip_f, chip_r,
    line, line_out,
    scan_f, scan_r,
    full_f, full_r,
    kv, gr,
    attn_l, gq_l, gk_l, gv_l,
    attn_s, attn_r, gq_s, gk_s, gv_s,
    perm_in, perm_out, order,
    in_sem, out_sem, send_sem, recv_sem,
):
    columns = xs * CORES
    owners = zs // 2
    sub = HALF // owners
    chunk = xs * sub
    width = q.shape[1]
    pairs = width // PAIR
    rows_y = GROUP // ys

    seq = lax.axis_index("seq")
    y = lax.axis_index("head")
    x = seq // (zs * CORES)
    z = (seq // CORES) % zs
    core = seq % CORES
    column = x * CORES + core
    even = z % 2 == 0

    def at_column(o):
        return (((o // CORES) * zs + z) * CORES + o % CORES, y)

    def at_z(zz):
        return ((x * zs + zz) * CORES + core, y)

    def at_y(yy):
        return (seq, yy)

    def rows(i, n):
        return pl.ds(pl.multiple_of(i * n, n), n)

    def cols(i, n):
        return pl.ds(pl.multiple_of(i * n, n), n)

    def send(src, dst, which, device):
        pltpu.make_async_remote_copy(
            src_ref=src, dst_ref=dst, send_sem=send_sem.at[which], recv_sem=recv_sem.at[which],
            device_id=device, device_id_type=MESH,
        ).start()

    def arrived(ref, which):
        pltpu.make_async_copy(ref, ref, recv_sem.at[which]).wait()

    def sent(ref, which):
        pltpu.make_async_copy(ref, ref, send_sem.at[which]).wait()

    G, P1F, P1R, P2, P3F, P3R, P4F, P4R, AT = range(9)

    loads = [
        pltpu.make_async_copy(src, dst, in_sem.at[i])
        for i, (src, dst) in enumerate(
            (
                (k_hbm, k), (v_hbm, v), (q_hbm, q),
                (g_hbm.at[:, cols(y, width)], g.at[rows(y, rows_y)]),
            )
        )
    ]
    for load in loads:
        load.start()

    barrier = pltpu.get_barrier_semaphore()
    peers = []
    for d in range(1, ys):
        peers.append(at_y((y + d) % ys))
    for d in range(1, columns):
        peers.append(at_column((column + d) % columns))
    for d in range(1, zs):
        peers.append(at_z((z + d) % zs))
    for peer in peers:
        pl.semaphore_signal(barrier, inc=1, device_id=peer, device_id_type=MESH)

    lane_low = iota((GROUP, PAIR), 1) < DH
    state_low = iota((DH, PAIR), 1) < DH

    def split(a):
        return jnp.concatenate([jnp.where(lane_low, a, 0), jnp.where(lane_low, 0, a)], axis=0)

    def beside(a):
        return jnp.concatenate([a[:GROUP], a[GROUP:]], axis=1)

    def diagonal(s):
        return jnp.concatenate([jnp.where(state_low, s, 0), jnp.where(state_low, 0, s)], axis=0)

    def pair_state(a, b):
        both = dot(a, b, TN)
        return jnp.where(state_low, both[:DH], both[DH:]).astype(BF16)

    positions = (seq * GROUP + iota((GROUP, PAIR), 0)).astype(F32)
    factor = 1.0 / jnp.sqrt(DH * (positions + 1.0))

    loads[0].wait()
    loads[1].wait()
    for p in range(pairs):
        c = slice(p * PAIR, (p + 1) * PAIR)
        state_f[p * DH:(p + 1) * DH, :] = pair_state(k[:, c], v[:, c])

    pl.semaphore_wait(barrier, len(peers))
    for d in range(1, ys):
        to = (y + d) % ys
        send(g_hbm.at[:, cols(to, width)], g.at[rows(y, rows_y)], G, at_y(to))

    def to_columns(src, dst, which):
        for d in range(1, columns):
            o = (column + d) % columns
            send(src.at[rows(o, HALF)], dst.at[rows(column, HALF)], which, at_column(o))
        dst[rows(column, HALF), :] = src[rows(column, HALF), :]

    to_columns(state_f, part_f, P1F)

    r, s = iota((xs * HALF, columns * HALF), 0), iota((xs * HALF, columns * HALF), 1)
    perm_in[...] = jnp.where(
        (r % sub == s % sub)
        & ((r // chunk) == (s // sub) % owners)
        & ((r // sub) % xs == s // (CORES * HALF)),
        1.0, 0.0).astype(BF16)
    r, s = iota((xs * HALF, xs * HALF), 0), iota((xs * HALF, xs * HALF), 1)
    perm_out[...] = jnp.where(
        (r % sub == s % sub)
        & ((s // chunk) == (r // sub) % owners)
        & ((s // sub) % xs == r // HALF),
        1.0, 0.0).astype(BF16)
    r, s = iota((zs * chunk, zs * chunk), 0), iota((zs * chunk, zs * chunk), 1)
    ahead = ((r // sub) % xs - (s // sub) % xs) * zs + r // chunk - s // chunk
    order[...] = jnp.where((r % sub == s % sub) & (ahead * (1 - 2 * (z % 2)) > 0), 1.0, 0.0).astype(BF16)

    causal = iota((2 * GROUP, GROUP), 0) % GROUP >= iota((2 * GROUP, GROUP), 1)
    causal_t = iota((GROUP, 2 * GROUP), 1) % GROUP >= iota((GROUP, 2 * GROUP), 0)

    loads[2].wait()

    def scaled(a):
        return (a.astype(F32) * factor).astype(BF16)

    def inside_forward():
        for p in range(pairs):
            c = slice(p * PAIR, (p + 1) * PAIR)
            scores = jnp.where(causal, dot(split(scaled(q[:, c])), k[:, c], NT), 0.0).astype(BF16)
            attn_l[:, c] = dot(beside(scores), split(v[:, c]))

    def inside_backward():
        for p in range(pairs):
            c = slice(p * PAIR, (p + 1) * PAIR)
            g_two, q_two = split(scaled(g[:, c])), split(q[:, c])
            grad_scores = jnp.where(causal, dot(g_two, v[:, c], NT), 0.0).astype(BF16)
            gq_l[:, c] = dot(beside(grad_scores), split(k[:, c]))
            grad_scores_t = jnp.where(causal_t, dot(v[:, c], g_two, NT), 0.0).astype(BF16)
            gk_l[:, c] = dot(grad_scores_t, q_two)
            plain_t = jnp.where(causal_t, dot(k[:, c], q_two, NT), 0.0).astype(BF16)
            gv_l[:, c] = dot(plain_t, g_two)

    def to_owners(part, chip, which, parity):
        arrived(part.at[pl.ds(0, (columns - 1) * HALF)], which)
        chip[...] = dot(perm_in[...], part[...]).astype(BF16)
        mine = z // 2
        for d in range(owners):
            o = (mine + d) % owners

            def go(o=o):
                send(chip.at[rows(o, chunk)], line.at[rows(z, chunk)], P2, at_z(2 * o + parity))

            if d:
                go()
            else:
                pl.when(z % 2 != parity)(go)

        @pl.when(z % 2 == parity)
        def _():
            line[rows(z, chunk), :] = chip[rows(mine, chunk), :]

    def own(scan, which):
        arrived(line.at[pl.ds(0, (zs - 1) * chunk)], P2)
        line_out[...] = dot(order[...], line[...]).astype(BF16)
        mine = z // 2
        for d in range(1, zs):
            to = (z + d) % zs
            send(line_out.at[rows(to, chunk)], scan.at[rows(mine, chunk)], which, at_z(to))
        scan[rows(mine, chunk), :] = line_out[rows(z, chunk), :]

    def back(scan, part, full, dst, which3, which4, parity):
        @pl.when(z % 2 == parity)
        def _():
            arrived(scan.at[pl.ds(0, (owners - 1) * chunk)], which3)

        @pl.when(z % 2 != parity)
        def _():
            arrived(scan, which3)

        outer = dot(perm_out[...], scan[...])
        for xx in range(xs):
            base = outer[xx * HALF:(xx + 1) * HALF]
            at = xx * CORES * HALF
            plain, more = (at, at + HALF) if parity == 0 else (at + HALF, at)
            full[plain:plain + HALF, :] = base.astype(BF16)
            full[more:more + HALF, :] = (base + part[plain:plain + HALF, :].astype(F32)).astype(BF16)
        to_columns(full, dst, which4)

    inside_forward()
    to_owners(part_f, chip_f, P1F, 0)

    loads[3].wait()
    arrived(g.at[pl.ds(0, (ys - 1) * rows_y)], G)
    for p in range(pairs):
        c = slice(p * PAIR, (p + 1) * PAIR)
        state_r[p * DH:(p + 1) * DH, :] = pair_state(q[:, c], scaled(g[:, c]))
    to_columns(state_r, part_r, P1R)

    pl.when(even)(functools.partial(own, scan_f, P3F))
    to_owners(part_r, chip_r, P1R, 1)
    inside_backward()
    back(scan_f, part_f, full_f, kv, P3F, P4F, 0)
    pl.when(jnp.logical_not(even))(functools.partial(own, scan_r, P3R))

    arrived(kv.at[pl.ds(0, (columns - 1) * HALF)], P4F)
    for p in range(pairs):
        c = slice(p * PAIR, (p + 1) * PAIR)
        state = diagonal(kv[p * DH:(p + 1) * DH, :])
        attn_s[:, c] = (attn_l[:, c] + dot(scaled(q[:, c]), state)).astype(BF16)
    for d in range(1, ys):
        to = (y + d) % ys
        send(attn_s.at[rows(to, rows_y)], attn_r.at[:, cols(y, width)], AT, at_y(to))
    attn_r[:, cols(y, width)] = attn_s[rows(y, rows_y), :]
    for p in range(pairs):
        c = slice(p * PAIR, (p + 1) * PAIR)
        state = diagonal(kv[p * DH:(p + 1) * DH, :])
        gq_s[:, c] = (gq_l[:, c] + dot(scaled(g[:, c]), state, NT)).astype(BF16)
    out_gq = pltpu.make_async_copy(gq_s, gq_o, out_sem.at[0])
    out_gq.start()

    back(scan_r, part_r, full_r, gr, P3R, P4R, 1)
    arrived(attn_r.at[:, pl.ds(0, (ys - 1) * width)], AT)
    out_attn = pltpu.make_async_copy(attn_r, attn_o, out_sem.at[1])
    out_attn.start()

    arrived(gr.at[pl.ds(0, (columns - 1) * HALF)], P4R)
    for p in range(pairs):
        c = slice(p * PAIR, (p + 1) * PAIR)
        state = diagonal(gr[p * DH:(p + 1) * DH, :])
        gk_s[:, c] = (gk_l[:, c] + dot(v[:, c], state, NT)).astype(BF16)
        gv_s[:, c] = (gv_l[:, c] + dot(k[:, c], state)).astype(BF16)
    out_gk = pltpu.make_async_copy(gk_s, gk_o, out_sem.at[2])
    out_gk.start()
    out_gv = pltpu.make_async_copy(gv_s, gv_o, out_sem.at[3])
    out_gv.start()

    sent(g.at[pl.ds(0, (ys - 1) * rows_y)], G)
    for which in (P1F, P1R, P4F, P4R):
        sent(kv.at[pl.ds(0, (columns - 1) * HALF)], which)
    sent(line.at[pl.ds(0, (2 * owners - 1) * chunk)], P2)

    @pl.when(even)
    def _():
        sent(line.at[pl.ds(0, (zs - 1) * chunk)], P3F)

    @pl.when(jnp.logical_not(even))
    def _():
        sent(line.at[pl.ds(0, (zs - 1) * chunk)], P3R)

    sent(attn_r.at[:, pl.ds(0, (ys - 1) * width)], AT)
    for out in (out_gq, out_attn, out_gk, out_gv):
        out.wait()


def shards(xs, zs, ys, query_rot, key_rot, value_rot, grad_out):
    tok, width = query_rot.shape
    columns = xs * CORES
    chunk = xs * (HALF // (zs // 2))
    state = pltpu.VMEM((columns * HALF, PAIR), BF16)
    block = pltpu.VMEM((tok, width), BF16)
    wide = pltpu.VMEM((tok, width), F32)
    half = pltpu.VMEM((xs * HALF, PAIR), BF16)
    line = pltpu.VMEM((zs * chunk, PAIR), BF16)
    any_spec = pl.BlockSpec(memory_space=pl.ANY)
    like = jax.ShapeDtypeStruct((tok, width), BF16)
    return pl.pallas_call(
        functools.partial(kernel, xs, zs, ys),
        out_shape=(jax.ShapeDtypeStruct(grad_out.shape, BF16), like, like, like),
        in_specs=[any_spec] * 4,
        out_specs=(any_spec,) * 4,
        scratch_shapes=[
            block, block, block, block,
            state, state,
            state, state,
            half, half,
            line, line,
            half, half,
            state, state,
            state, state,
            wide, wide, wide, wide,
            block, pltpu.VMEM(grad_out.shape, BF16), block, block, block,
            pltpu.VMEM((xs * HALF, columns * HALF), BF16),
            pltpu.VMEM((xs * HALF, xs * HALF), BF16),
            pltpu.VMEM((zs * chunk, zs * chunk), BF16),
            pltpu.SemaphoreType.DMA((4,)),
            pltpu.SemaphoreType.DMA((4,)),
            pltpu.SemaphoreType.DMA((9,)),
            pltpu.SemaphoreType.DMA((9,)),
        ],
        compiler_params=pltpu.CompilerParams(
            collective_id=0, has_side_effects=True, vmem_limit_bytes=32 * 2**20
        ),
    )(query_rot, key_rot, value_rot, grad_out)


def solution(mesh, xs=XS, zs=ZS):
    in_specs = (P("seq", "head"), P("seq", "head"), P("seq", "head"), P(("seq", "head"), None))
    out_specs = (P(("seq", "head"), None), P("seq", "head"), P("seq", "head"), P("seq", "head"))
    return jax.shard_map(
        functools.partial(shards, xs, zs, mesh.shape["head"]),
        mesh=mesh, in_specs=in_specs, out_specs=out_specs, check_vma=False,
    )
```

```python
import functools

import jax
import jax.numpy as jnp
from jax import lax
from jax.experimental import pallas as pl
from jax.experimental.pallas import tpu as pltpu
from jax.sharding import PartitionSpec as P

DH = 64
GROUP = 128
XS = 4
ZS = 16
CORES = 2
PAIR = 2 * DH
HALF = DH // CORES
FORWARD_AT = (0, 2, 4, 15)
BACKWARD_AT = (1, 3, 5, 14)
BACK_ORDER = (0, 1, 2, 3, 4, 15, 5, 14, 6, 13, 7, 12, 8, 11, 9, 10)
MESH = pl.DeviceIdType.MESH
F32 = jnp.float32
BF16 = jnp.bfloat16

NN = (((1,), (0,)), ((), ()))
NT = (((1,), (1,)), ((), ()))
TN = (((0,), (0,)), ((), ()))
G, CF, CR, OUT, TOT, BF, BR, AT = range(8)


def dot(a, b, dims=NN):
    return lax.dot_general(a, b, dims, preferred_element_type=F32)


def iota(shape, dim):
    return lax.broadcasted_iota(jnp.int32, shape, dim)


def kernel(
    xs, zs, ys, forward_at, backward_at, back_order,
    q_hbm, k_hbm, v_hbm, g_hbm,
    attn_o, gq_o, gk_o, gv_o,
    q, k, v, g,
    own_f, own_r, sib_f, sib_r,
    chip_f, chip_r,
    line, part, line_out,
    totals,
    scan_f, scan_r,
    attn_l, gq_l, gk_l, gv_l,
    attn_s, attn_r, gq_s, gk_s, gv_s,
    in_sem, out_sem, send_sem, recv_sem,
):
    width = q.shape[1]
    pairs = width // PAIR
    half = pairs * HALF
    chunk = half // len(forward_at)
    rows_y = GROUP // ys

    seq = lax.axis_index("seq")
    y = lax.axis_index("head")
    x = seq // (zs * CORES)
    z = (seq // CORES) % zs
    core = seq % CORES

    def device(xx, zz, cc):
        return ((xx * zs + zz) * CORES + cc, y)

    def among(zz, places):
        found = zz == places[0]
        for place in places[1:]:
            found = jnp.logical_or(found, zz == place)
        return found

    def aligned(i, n):
        return pl.ds(pl.multiple_of(i * n, n), n)

    def send(src, dst, which, to):
        pltpu.make_async_remote_copy(
            src_ref=src, dst_ref=dst, send_sem=send_sem.at[which], recv_sem=recv_sem.at[which],
            device_id=to, device_id_type=MESH,
        ).start()

    def arrived(ref, which):
        pltpu.make_async_copy(ref, ref, recv_sem.at[which]).wait()

    def sent(ref, which):
        pltpu.make_async_copy(ref, ref, send_sem.at[which]).wait()

    barrier = pltpu.get_barrier_semaphore()
    both = forward_at + backward_at
    owner = among(z, both)
    sibling = device(x, z, 1 - core)

    def greet(to):
        pl.semaphore_signal(barrier, inc=1, device_id=to, device_id_type=MESH)

    for zz in range(zs):
        for cc in range(CORES):
            near = jnp.logical_and(z == zz, core == cc)
            if zz in both:
                meet = jnp.logical_not(near)
            else:
                meet = jnp.logical_and(jnp.logical_or(owner, z == zz), jnp.logical_not(near))
            pl.when(meet)(functools.partial(greet, device(x, zz, cc)))
    for d in range(1, ys):
        greet((seq, (y + d) % ys))
    for d in range(1, xs):
        greet(device((x + d) % xs, z, core))
    greeted = ys - 1 + xs - 1 + jnp.where(owner, CORES * zs - 1, CORES * len(both) + 1)

    loads = [
        pltpu.make_async_copy(src, dst, in_sem.at[i])
        for i, (src, dst) in enumerate(
            (
                (k_hbm, k), (v_hbm, v), (q_hbm, q),
                (g_hbm.at[:, aligned(y, width)], g.at[aligned(y, rows_y)]),
            )
        )
    ]
    for load in loads:
        load.start()

    lane_low = iota((GROUP, PAIR), 1) < DH
    state_low = iota((DH, PAIR), 1) < DH

    def split(a):
        return jnp.concatenate([jnp.where(lane_low, a, 0), jnp.where(lane_low, 0, a)], axis=0)

    def beside(a):
        return jnp.concatenate([a[:GROUP], a[GROUP:]], axis=1)

    def diagonal(s):
        return jnp.concatenate([jnp.where(state_low, s, 0), jnp.where(state_low, 0, s)], axis=0)

    def columns(p):
        return slice(p * PAIR, (p + 1) * PAIR)

    def at(h, p):
        return slice(h * half + p * HALF, h * half + (p + 1) * HALF)

    def pair_state(own, p, a, b):
        product = dot(a, b, TN)
        state = jnp.where(state_low, product[:DH], product[DH:])
        for h in range(CORES):
            own[at(h, p), :] = state[h * HALF:(h + 1) * HALF]

    positions = (seq * GROUP + iota((GROUP, PAIR), 0)).astype(F32)
    factor = 1.0 / jnp.sqrt(DH * (positions + 1.0))

    def scaled(a):
        return (a.astype(F32) * factor).astype(BF16)

    def to_owners(own, sib, chip, which, places):
        arrived(sib, which)
        mine = aligned(core, half)
        chip[...] = (own[mine, :] + sib[mine, :]).astype(BF16)
        for i, place in enumerate(places):
            piece = chip.at[pl.ds(i * chunk, chunk)]

            @pl.when(z != place)
            def _(piece=piece, place=place):
                send(piece, line.at[aligned(z, chunk)], OUT, device(x, place, core))

            @pl.when(z == place)
            def _(i=i, place=place):
                line[place * chunk:(place + 1) * chunk, :] = chip[i * chunk:(i + 1) * chunk, :]

    def own_chunk(scan, which, i, place, backward):
        arrived(line.at[pl.ds(0, (zs - 1) * chunk)], OUT)
        total = None
        for step in range(zs):
            zz = zs - 1 - step if backward else step
            piece = line[zz * chunk:(zz + 1) * chunk, :].astype(F32)
            part[zz * chunk:(zz + 1) * chunk, :] = jnp.zeros_like(piece) if total is None else total
            total = piece if total is None else total + piece
        totals[aligned(x, chunk), :] = total
        for d in range(1, xs):
            send(totals.at[aligned(x, chunk)], totals.at[aligned(x, chunk)], TOT, device((x + d) % xs, place, core))
        arrived(totals.at[pl.ds(0, (xs - 1) * chunk)], TOT)
        base = jnp.zeros_like(total)
        for xx in range(xs):
            counts = xx > x if backward else xx < x
            base = base + jnp.where(counts, totals[xx * chunk:(xx + 1) * chunk, :], 0.0)
        for zz in range(zs):
            line_out[zz * chunk:(zz + 1) * chunk, :] = (part[zz * chunk:(zz + 1) * chunk, :] + base).astype(BF16)
        home = pl.ds(pl.multiple_of(core * half + i * chunk, chunk), chunk)
        for zz in back_order:
            piece = line_out.at[pl.ds(zz * chunk, chunk)]
            if zz == place:
                send(piece, scan.at[home], which, sibling)
                scan[home, :] = line_out[zz * chunk:(zz + 1) * chunk, :]
            else:
                for cc in range(CORES):
                    send(piece, scan.at[home], which, device(x, zz, cc))

    def own_one(scan, which, places, backward):
        for i, place in enumerate(places):
            pl.when(z == place)(functools.partial(own_chunk, scan, which, i, place, backward))

    def came_back(scan, which, places):
        mine = among(z, places)

        @pl.when(mine)
        def _():
            arrived(scan.at[pl.ds(0, CORES * half - chunk)], which)

        @pl.when(jnp.logical_not(mine))
        def _():
            arrived(scan, which)

    def state_of(scan, sib, weight, p):
        rows = [scan[at(h, p), :].astype(F32) + weight * sib[at(h, p), :] for h in range(CORES)]
        return diagonal(jnp.concatenate(rows, axis=0)).astype(BF16)

    loads[0].wait()
    loads[1].wait()
    for p in range(pairs):
        pair_state(own_f, p, k[:, columns(p)], v[:, columns(p)])
    pl.semaphore_wait(barrier, greeted)
    for d in range(1, ys):
        to = (y + d) % ys
        send(g_hbm.at[:, aligned(to, width)], g.at[aligned(y, rows_y)], G, (seq, to))
    send(own_f, sib_f, CF, sibling)

    causal = iota((2 * GROUP, GROUP), 0) % GROUP >= iota((2 * GROUP, GROUP), 1)
    causal_t = iota((GROUP, 2 * GROUP), 1) % GROUP >= iota((GROUP, 2 * GROUP), 0)
    to_owners(own_f, sib_f, chip_f, CF, forward_at)

    loads[2].wait()
    for p in range(pairs):
        c = columns(p)
        scores = jnp.where(causal, dot(split(scaled(q[:, c])), k[:, c], NT), 0.0).astype(BF16)
        attn_l[:, c] = dot(beside(scores), split(v[:, c]))

    loads[3].wait()
    arrived(g.at[pl.ds(0, (ys - 1) * rows_y)], G)
    for p in range(pairs):
        pair_state(own_r, p, q[:, columns(p)], scaled(g[:, columns(p)]))
    send(own_r, sib_r, CR, sibling)
    to_owners(own_r, sib_r, chip_r, CR, backward_at)

    for p in range(pairs):
        c = columns(p)
        g_two, q_two = split(scaled(g[:, c])), split(q[:, c])
        grad_scores = jnp.where(causal, dot(g_two, v[:, c], NT), 0.0).astype(BF16)
        gq_l[:, c] = dot(beside(grad_scores), split(k[:, c]))
        grad_scores_t = jnp.where(causal_t, dot(v[:, c], g_two, NT), 0.0).astype(BF16)
        gk_l[:, c] = dot(grad_scores_t, q_two)
        plain_t = jnp.where(causal_t, dot(k[:, c], q_two, NT), 0.0).astype(BF16)
        gv_l[:, c] = dot(plain_t, g_two)

    own_one(scan_f, BF, forward_at, False)
    own_one(scan_r, BR, backward_at, True)

    after = core.astype(F32)
    came_back(scan_f, BF, forward_at)
    for p in range(pairs):
        c = columns(p)
        state = state_of(scan_f, sib_f, after, p)
        attn_s[:, c] = (attn_l[:, c] + dot(scaled(q[:, c]), state)).astype(BF16)
    for d in range(1, ys):
        to = (y + d) % ys
        send(attn_s.at[aligned(to, rows_y)], attn_r.at[:, aligned(y, width)], AT, (seq, to))
    attn_r[:, aligned(y, width)] = attn_s[aligned(y, rows_y), :]
    for p in range(pairs):
        c = columns(p)
        state = state_of(scan_f, sib_f, after, p)
        gq_s[:, c] = (gq_l[:, c] + dot(scaled(g[:, c]), state, NT)).astype(BF16)
    out_gq = pltpu.make_async_copy(gq_s, gq_o, out_sem.at[0])
    out_gq.start()

    came_back(scan_r, BR, backward_at)
    for p in range(pairs):
        c = columns(p)
        state = state_of(scan_r, sib_r, 1.0 - after, p)
        gk_s[:, c] = (gk_l[:, c] + dot(v[:, c], state, NT)).astype(BF16)
        gv_s[:, c] = (gv_l[:, c] + dot(k[:, c], state)).astype(BF16)
    out_gk = pltpu.make_async_copy(gk_s, gk_o, out_sem.at[1])
    out_gk.start()
    out_gv = pltpu.make_async_copy(gv_s, gv_o, out_sem.at[2])
    out_gv.start()

    arrived(attn_r.at[:, pl.ds(0, (ys - 1) * width)], AT)
    out_attn = pltpu.make_async_copy(attn_r, attn_o, out_sem.at[3])
    out_attn.start()

    sent(g.at[pl.ds(0, (ys - 1) * rows_y)], G)
    sent(own_f, CF)
    sent(own_r, CR)
    sent(attn_r.at[:, pl.ds(0, (ys - 1) * width)], AT)

    @pl.when(jnp.logical_not(owner))
    def _():
        sent(chip_f, OUT)
        sent(chip_r, OUT)

    @pl.when(owner)
    def _():
        sent(chip_f, OUT)
        sent(chip_r.at[pl.ds(0, half - chunk)], OUT)
        sent(totals.at[pl.ds(0, (xs - 1) * chunk)], TOT)

    for places, which in ((forward_at, BF), (backward_at, BR)):

        @pl.when(among(z, places))
        def _(which=which):
            sent(line_out, which)
            sent(line_out.at[pl.ds(0, (zs - 1) * chunk)], which)

    for out in (out_gq, out_gk, out_gv, out_attn):
        out.wait()


def shards(xs, zs, ys, forward_at, backward_at, back_order, query_rot, key_rot, value_rot, grad_out):
    tok, width = query_rot.shape
    half = width // PAIR * HALF
    chunk = half // len(forward_at)
    block = pltpu.VMEM((tok, width), BF16)
    wide = pltpu.VMEM((tok, width), F32)
    state = pltpu.VMEM((CORES * half, PAIR), F32)
    chip = pltpu.VMEM((half, PAIR), BF16)
    line = pltpu.VMEM((zs * chunk, PAIR), BF16)
    scan = pltpu.VMEM((CORES * half, PAIR), BF16)
    like = jax.ShapeDtypeStruct((tok, width), BF16)
    return pl.pallas_call(
        functools.partial(kernel, xs, zs, ys, forward_at, backward_at, back_order),
        out_shape=(jax.ShapeDtypeStruct(grad_out.shape, BF16), like, like, like),
        in_specs=[pl.BlockSpec(memory_space=pltpu.HBM)] * 4,
        out_specs=(pl.BlockSpec(memory_space=pl.ANY),) * 4,
        scratch_shapes=[
            block, block, block, block,
            state, state, state, state,
            chip, chip,
            line, pltpu.VMEM((zs * chunk, PAIR), F32), line,
            pltpu.VMEM((xs * chunk, PAIR), F32),
            scan, scan,
            wide, wide, wide, wide,
            block, pltpu.VMEM(grad_out.shape, BF16), block, block, block,
            pltpu.SemaphoreType.DMA((4,)),
            pltpu.SemaphoreType.DMA((4,)),
            pltpu.SemaphoreType.DMA((8,)),
            pltpu.SemaphoreType.DMA((8,)),
        ],
        compiler_params=pltpu.CompilerParams(
            collective_id=0, has_side_effects=True, vmem_limit_bytes=63 * 2**20
        ),
    )(query_rot, key_rot, value_rot, grad_out)


def solution(mesh, xs=XS, zs=ZS, forward_at=FORWARD_AT, backward_at=BACKWARD_AT, back_order=BACK_ORDER):
    in_specs = (P("seq", "head"), P("seq", "head"), P("seq", "head"), P(("seq", "head"), None))
    out_specs = (P(("seq", "head"), None), P("seq", "head"), P("seq", "head"), P("seq", "head"))
    return jax.shard_map(
        functools.partial(shards, xs, zs, mesh.shape["head"], forward_at, backward_at, back_order),
        mesh=mesh, in_specs=in_specs, out_specs=out_specs, check_vma=False,
    )
```

```python
import functools

import jax
import jax.numpy as jnp
from jax import lax
from jax.experimental import pallas as pl
from jax.experimental.pallas import tpu as pltpu
from jax.sharding import PartitionSpec as P

DH = 64
GROUP = 128
XS = 4
ZS = 16
CORES = 2
PAIR = 2 * DH
HALF = DH // CORES
FORWARD_AT = (12, 14, 0, 2)
BACKWARD_AT = (13, 15, 1, 3)
BACK_ORDER = (0, 1, 2, 15, 3, 14, 4, 13, 5, 12, 6, 11, 7, 10, 8, 9)
MESH = pl.DeviceIdType.MESH
F32 = jnp.float32
BF16 = jnp.bfloat16

NN = (((1,), (0,)), ((), ()))
NT = (((1,), (1,)), ((), ()))
TN = (((0,), (0,)), ((), ()))
G, CF, CR, OUT, TOT, BF, BR, AT = range(8)


def dot(a, b, dims=NN):
    return lax.dot_general(a, b, dims, preferred_element_type=F32)


def iota(shape, dim):
    return lax.broadcasted_iota(jnp.int32, shape, dim)


def kernel(
    xs, zs, ys, forward_at, backward_at, back_order,
    q_hbm, k_hbm, v_hbm, g_hbm,
    attn_r, gq_s, gk_s, gv_s,
    q, k, v, g_in, g,
    own_f, own_r, sib_f, sib_r,
    chip_f, chip_r,
    line, part, line_out,
    totals,
    scan_f, scan_r,
    attn_l, gq_l, gk_l, gv_l,
    attn_s,
    in_sem, send_sem, recv_sem,
):
    width = q.shape[1]
    pairs = width // PAIR
    half = pairs * HALF
    chunk = half // len(forward_at)
    rows_y = GROUP // ys

    seq = lax.axis_index("seq")
    y = lax.axis_index("head")
    x = seq // (zs * CORES)
    z = (seq // CORES) % zs
    core = seq % CORES

    def device(xx, zz, cc):
        return ((xx * zs + zz) * CORES + cc, y)

    def among(zz, places):
        found = zz == places[0]
        for place in places[1:]:
            found = jnp.logical_or(found, zz == place)
        return found

    def aligned(i, n):
        return pl.ds(pl.multiple_of(i * n, n), n)

    def send(src, dst, which, to):
        pltpu.make_async_remote_copy(
            src_ref=src, dst_ref=dst, send_sem=send_sem.at[which], recv_sem=recv_sem.at[which],
            device_id=to, device_id_type=MESH,
        ).start()

    def arrived(ref, which):
        pltpu.make_async_copy(ref, ref, recv_sem.at[which]).wait()

    def sent(ref, which):
        pltpu.make_async_copy(ref, ref, send_sem.at[which]).wait()

    barrier = pltpu.get_barrier_semaphore()
    both = forward_at + backward_at
    owner = among(z, both)
    sibling = device(x, z, 1 - core)

    def greet(to):
        pl.semaphore_signal(barrier, inc=1, device_id=to, device_id_type=MESH)

    for d in range(1, ys):
        greet((seq, (y + d) % ys))
    for d in range(1, xs):
        greet(device((x + d) % xs, z, core))
    greet(sibling)
    for zz in range(zs):
        for cc in range(CORES):
            meet = jnp.logical_and(True if zz in both else owner, z != zz)
            pl.when(meet)(functools.partial(greet, device(x, zz, cc)))
    greeted = ys - 1 + xs - 1 + 1 + CORES * jnp.where(owner, zs - 1, len(both))

    loads = [
        pltpu.make_async_copy(src, dst, in_sem.at[i])
        for i, (src, dst) in enumerate(
            (
                (k_hbm, k), (v_hbm, v), (g_hbm, g_in), (q_hbm, q),
            )
        )
    ]
    for load in loads:
        load.start()

    lane_low = iota((GROUP, PAIR), 1) < DH
    state_low = iota((DH, PAIR), 1) < DH

    def split(a):
        return jnp.concatenate([jnp.where(lane_low, a, 0), jnp.where(lane_low, 0, a)], axis=0)

    def beside(a):
        return jnp.concatenate([a[:GROUP], a[GROUP:]], axis=1)

    def diagonal(s):
        return jnp.concatenate([jnp.where(state_low, s, 0), jnp.where(state_low, 0, s)], axis=0)

    def columns(p):
        return slice(p * PAIR, (p + 1) * PAIR)

    def at(h, p):
        return slice(h * half + p * HALF, h * half + (p + 1) * HALF)

    def pair_state(own, p, a, b):
        product = dot(a, b, TN)
        state = jnp.where(state_low, product[:DH], product[DH:])
        for h in range(CORES):
            own[at(h, p), :] = state[h * HALF:(h + 1) * HALF]

    positions = (seq * GROUP + iota((GROUP, PAIR), 0)).astype(F32)
    factor = 1.0 / jnp.sqrt(DH * (positions + 1.0))

    def scaled(a):
        return (a.astype(F32) * factor).astype(BF16)

    def to_owners(own, sib, chip, which, places):
        arrived(sib, which)
        mine = aligned(core, half)
        chip[...] = (own[mine, :] + sib[mine, :]).astype(BF16)
        for i, place in enumerate(places):
            piece = chip.at[pl.ds(i * chunk, chunk)]

            @pl.when(z != place)
            def _(piece=piece, place=place):
                send(piece, line.at[aligned(z, chunk)], OUT, device(x, place, core))

            @pl.when(z == place)
            def _(i=i, place=place):
                line[place * chunk:(place + 1) * chunk, :] = chip[i * chunk:(i + 1) * chunk, :]

    def own_chunk(scan, which, i, place, backward):
        arrived(line.at[pl.ds(0, (zs - 1) * chunk)], OUT)
        total = None
        for step in range(zs):
            zz = zs - 1 - step if backward else step
            piece = line[zz * chunk:(zz + 1) * chunk, :].astype(F32)
            part[zz * chunk:(zz + 1) * chunk, :] = jnp.zeros_like(piece) if total is None else total
            total = piece if total is None else total + piece
        totals[aligned(x, chunk), :] = total
        for xx in range(xs):
            def pass_on(xx=xx):
                send(totals.at[aligned(x, chunk)], totals.at[aligned(x, chunk)], TOT, device(xx, place, core))

            pl.when(xx < x if backward else xx > x)(pass_on)
        waits = (lambda xx: xs - 1 - xx) if backward else (lambda xx: xx)
        for xx in range(xs):
            if waits(xx):

                @pl.when(x == xx)
                def _(n=waits(xx)):
                    arrived(totals.at[pl.ds(0, n * chunk)], TOT)

        base = jnp.zeros_like(total)
        for xx in range(xs):
            counts = xx > x if backward else xx < x
            base = base + jnp.where(counts, totals[xx * chunk:(xx + 1) * chunk, :], 0.0)
        for zz in range(zs):
            line_out[zz * chunk:(zz + 1) * chunk, :] = (part[zz * chunk:(zz + 1) * chunk, :] + base).astype(BF16)
        home = pl.ds(pl.multiple_of(core * half + i * chunk, chunk), chunk)
        for zz in back_order:
            piece = line_out.at[pl.ds(zz * chunk, chunk)]
            if zz == place:
                send(piece, scan.at[home], which, sibling)
                scan[home, :] = line_out[zz * chunk:(zz + 1) * chunk, :]
            else:
                for cc in range(CORES):
                    send(piece, scan.at[home], which, device(x, zz, cc))

    def own_one(scan, which, places, backward):
        for i, place in enumerate(places):
            pl.when(z == place)(functools.partial(own_chunk, scan, which, i, place, backward))

    def came_back(scan, which, places):
        mine = among(z, places)

        @pl.when(mine)
        def _():
            arrived(scan.at[pl.ds(0, CORES * half - chunk)], which)

        @pl.when(jnp.logical_not(mine))
        def _():
            arrived(scan, which)

    def state_of(scan, sib, weight, p):
        rows = [scan[at(h, p), :].astype(F32) + weight * sib[at(h, p), :] for h in range(CORES)]
        return diagonal(jnp.concatenate(rows, axis=0)).astype(BF16)

    loads[0].wait()
    loads[1].wait()
    for p in range(pairs):
        pair_state(own_f, p, k[:, columns(p)], v[:, columns(p)])
    loads[2].wait()
    pl.semaphore_wait(barrier, greeted)
    for d in range(1, ys):
        to = (y + d) % ys
        send(g_in.at[:, aligned(to, width)], g.at[aligned(y, rows_y)], G, (seq, to))
    send(own_f, sib_f, CF, sibling)
    g[aligned(y, rows_y), :] = g_in[:, aligned(y, width)]

    causal = iota((2 * GROUP, GROUP), 0) % GROUP >= iota((2 * GROUP, GROUP), 1)
    causal_t = iota((GROUP, 2 * GROUP), 1) % GROUP >= iota((GROUP, 2 * GROUP), 0)
    to_owners(own_f, sib_f, chip_f, CF, forward_at)

    loads[3].wait()
    for p in range(pairs):
        c = columns(p)
        scores = jnp.where(causal, dot(split(scaled(q[:, c])), k[:, c], NT), 0.0).astype(BF16)
        attn_l[:, c] = dot(beside(scores), split(v[:, c]))

    arrived(g.at[pl.ds(0, (ys - 1) * rows_y)], G)
    for p in range(pairs):
        pair_state(own_r, p, q[:, columns(p)], scaled(g[:, columns(p)]))
    send(own_r, sib_r, CR, sibling)
    to_owners(own_r, sib_r, chip_r, CR, backward_at)

    for p in range(pairs):
        c = columns(p)
        g_two, q_two = split(scaled(g[:, c])), split(q[:, c])
        grad_scores = jnp.where(causal, dot(g_two, v[:, c], NT), 0.0).astype(BF16)
        gq_l[:, c] = dot(beside(grad_scores), split(k[:, c]))
        grad_scores_t = jnp.where(causal_t, dot(v[:, c], g_two, NT), 0.0).astype(BF16)
        gk_l[:, c] = dot(grad_scores_t, q_two)
        plain_t = jnp.where(causal_t, dot(k[:, c], q_two, NT), 0.0).astype(BF16)
        gv_l[:, c] = dot(plain_t, g_two)

    own_one(scan_f, BF, forward_at, False)
    own_one(scan_r, BR, backward_at, True)

    after = core.astype(F32)
    came_back(scan_f, BF, forward_at)
    for p in range(pairs):
        c = columns(p)
        state = state_of(scan_f, sib_f, after, p)
        attn_s[:, c] = (attn_l[:, c] + dot(scaled(q[:, c]), state)).astype(BF16)
    for d in range(1, ys):
        to = (y + d) % ys
        send(attn_s.at[aligned(to, rows_y)], attn_r.at[:, aligned(y, width)], AT, (seq, to))
    attn_r[:, aligned(y, width)] = attn_s[aligned(y, rows_y), :]
    for p in range(pairs):
        c = columns(p)
        state = state_of(scan_f, sib_f, after, p)
        gq_s[:, c] = (gq_l[:, c] + dot(scaled(g[:, c]), state, NT)).astype(BF16)

    came_back(scan_r, BR, backward_at)
    for p in range(pairs):
        c = columns(p)
        state = state_of(scan_r, sib_r, 1.0 - after, p)
        gk_s[:, c] = (gk_l[:, c] + dot(v[:, c], state, NT)).astype(BF16)
        gv_s[:, c] = (gv_l[:, c] + dot(k[:, c], state)).astype(BF16)

    arrived(attn_r.at[:, pl.ds(0, (ys - 1) * width)], AT)

    sent(g.at[pl.ds(0, (ys - 1) * rows_y)], G)
    sent(own_f, CF)
    sent(own_r, CR)
    sent(attn_r.at[:, pl.ds(0, (ys - 1) * width)], AT)

    @pl.when(jnp.logical_not(owner))
    def _():
        sent(chip_f, OUT)
        sent(chip_r, OUT)

    @pl.when(owner)
    def _():
        sent(chip_f, OUT)
        sent(chip_r.at[pl.ds(0, half - chunk)], OUT)

    for places, which in ((forward_at, BF), (backward_at, BR)):

        @pl.when(among(z, places))
        def _(which=which):
            sent(line_out, which)
            sent(line_out.at[pl.ds(0, (zs - 1) * chunk)], which)
            for xx in range(xs):
                n = xx if which == BR else xs - 1 - xx
                if n:
                    pl.when(x == xx)(functools.partial(sent, totals.at[pl.ds(0, n * chunk)], TOT))


def write_out(*refs):
    copies = [pltpu.make_async_copy(refs[i], refs[4 + i], refs[8].at[i]) for i in range(4)]
    for copy in copies:
        copy.start()
    for copy in copies:
        copy.wait()


def shards(xs, zs, ys, forward_at, backward_at, back_order, query_rot, key_rot, value_rot, grad_out):
    tok, width = query_rot.shape
    half = width // PAIR * HALF
    chunk = half // len(forward_at)
    block = pltpu.VMEM((tok, width), BF16)
    wide = pltpu.VMEM((tok, width), F32)
    state = pltpu.VMEM((CORES * half, PAIR), F32)
    chip = pltpu.VMEM((half, PAIR), BF16)
    line = pltpu.VMEM((zs * chunk, PAIR), BF16)
    scan = pltpu.VMEM((CORES * half, PAIR), BF16)
    operands = [pltpu.with_memory_space_constraint(a, pltpu.HBM) for a in (query_rot, key_rot, value_rot, grad_out)]
    results = pl.pallas_call(
        functools.partial(kernel, xs, zs, ys, forward_at, backward_at, back_order),
        out_shape=(pltpu.VMEM(grad_out.shape, BF16), block, block, block),
        in_specs=[pl.BlockSpec(memory_space=pltpu.HBM)] * 4,
        out_specs=(pl.BlockSpec(memory_space=pltpu.VMEM),) * 4,
        scratch_shapes=[
            block, block, block, pltpu.VMEM(grad_out.shape, BF16), block,
            state, state, state, state,
            chip, chip,
            line, pltpu.VMEM((zs * chunk, PAIR), F32), line,
            pltpu.VMEM((xs * chunk, PAIR), F32),
            scan, scan,
            wide, wide, wide, wide,
            block,
            pltpu.SemaphoreType.DMA((4,)),
            pltpu.SemaphoreType.DMA((8,)),
            pltpu.SemaphoreType.DMA((8,)),
        ],
        compiler_params=pltpu.CompilerParams(
            collective_id=0, has_side_effects=True, vmem_limit_bytes=32 * 2**20
        ),
    )(*operands)
    return pl.pallas_call(
        write_out,
        out_shape=tuple(jax.ShapeDtypeStruct(a.shape, a.dtype) for a in results),
        in_specs=[pl.BlockSpec(memory_space=pltpu.VMEM)] * 4,
        out_specs=(pl.BlockSpec(memory_space=pltpu.HBM),) * 4,
        scratch_shapes=[pltpu.SemaphoreType.DMA((4,))],
    )(*[pltpu.with_memory_space_constraint(a, pltpu.VMEM) for a in results])


def solution(mesh, xs=XS, zs=ZS, forward_at=FORWARD_AT, backward_at=BACKWARD_AT, back_order=BACK_ORDER):
    in_specs = (P("seq", "head"), P("seq", "head"), P("seq", "head"), P(("seq", "head"), None))
    out_specs = (P(("seq", "head"), None), P("seq", "head"), P("seq", "head"), P("seq", "head"))
    return jax.shard_map(
        functools.partial(shards, xs, zs, mesh.shape["head"], forward_at, backward_at, back_order),
        mesh=mesh, in_specs=in_specs, out_specs=out_specs, check_vma=False,
    )
```

```python
import functools

import jax
import jax.numpy as jnp
from jax import lax
from jax.experimental import pallas as pl
from jax.experimental.pallas import tpu as pltpu
from jax.sharding import PartitionSpec as P

DH = 64
GROUP = 128
XS = 4
ZS = 16
CORES = 2
PAIR = 2 * DH
HALF = DH // CORES
FORWARD_AT = (12, 14, 0, 2)
BACKWARD_AT = (13, 15, 1, 3)
BACK_ORDER = (0, 1, 2, 15, 3, 14, 4, 13, 5, 12, 6, 11, 7, 10, 8, 9)
MESH = pl.DeviceIdType.MESH
F32 = jnp.float32
BF16 = jnp.bfloat16

NN = (((1,), (0,)), ((), ()))
NT = (((1,), (1,)), ((), ()))
TN = (((0,), (0,)), ((), ()))
G, CF, CR, CF2, CR2, OUT, TOT, BF, BR, AT = range(10)


def dot(a, b, dims=NN):
    return lax.dot_general(a, b, dims, preferred_element_type=F32)


def iota(shape, dim):
    return lax.broadcasted_iota(jnp.int32, shape, dim)


def kernel(
    xs, zs, ys, forward_at, backward_at, back_order,
    q_hbm, k_hbm, v_hbm, g_hbm,
    attn_r, gq_s, gk_s, gv_s,
    q, k, v, g_in, g,
    own_f, own_r, sib_f, sib_r,
    chip_f, chip_r,
    line, part, line_out,
    totals,
    scan_f, scan_r,
    attn_l, gq_l, gk_l, gv_l,
    attn_s,
    in_sem, send_sem, recv_sem,
):
    width = q.shape[1]
    pairs = width // PAIR
    half = pairs * HALF
    chunk = half // len(forward_at)
    rows_y = GROUP // ys

    seq = lax.axis_index("seq")
    y = lax.axis_index("head")
    x = seq // (zs * CORES)
    z = (seq // CORES) % zs
    core = seq % CORES

    def device(xx, zz, cc):
        return ((xx * zs + zz) * CORES + cc, y)

    def among(zz, places):
        found = zz == places[0]
        for place in places[1:]:
            found = jnp.logical_or(found, zz == place)
        return found

    def aligned(i, n):
        return pl.ds(pl.multiple_of(i * n, n), n)

    def send(src, dst, which, to):
        pltpu.make_async_remote_copy(
            src_ref=src, dst_ref=dst, send_sem=send_sem.at[which], recv_sem=recv_sem.at[which],
            device_id=to, device_id_type=MESH,
        ).start()

    def arrived(ref, which):
        pltpu.make_async_copy(ref, ref, recv_sem.at[which]).wait()

    def sent(ref, which):
        pltpu.make_async_copy(ref, ref, send_sem.at[which]).wait()

    barrier = pltpu.get_barrier_semaphore()
    both = forward_at + backward_at
    owner = among(z, both)
    sibling = device(x, z, 1 - core)

    def greet(to):
        pl.semaphore_signal(barrier, inc=1, device_id=to, device_id_type=MESH)

    for d in range(1, ys):
        greet((seq, (y + d) % ys))
    for d in range(1, xs):
        greet(device((x + d) % xs, z, core))
    greet(sibling)
    for zz in range(zs):
        for cc in range(CORES):
            meet = jnp.logical_and(True if zz in both else owner, z != zz)
            pl.when(meet)(functools.partial(greet, device(x, zz, cc)))
    greeted = ys - 1 + xs - 1 + 1 + CORES * jnp.where(owner, zs - 1, len(both))

    loads = [
        pltpu.make_async_copy(src, dst, in_sem.at[i])
        for i, (src, dst) in enumerate(
            (
                (g_hbm, g_in), (k_hbm, k), (v_hbm, v), (q_hbm, q),
            )
        )
    ]
    for load in loads:
        load.start()

    lane_low = iota((GROUP, PAIR), 1) < DH
    state_low = iota((DH, PAIR), 1) < DH

    def split(a):
        return jnp.concatenate([jnp.where(lane_low, a, 0), jnp.where(lane_low, 0, a)], axis=0)

    def beside(a):
        return jnp.concatenate([a[:GROUP], a[GROUP:]], axis=1)

    def diagonal(s):
        return jnp.concatenate([jnp.where(state_low, s, 0), jnp.where(state_low, 0, s)], axis=0)

    def columns(p):
        return slice(p * PAIR, (p + 1) * PAIR)

    def at(h, p):
        return slice(h * half + p * HALF, h * half + (p + 1) * HALF)

    def pair_state(own, p, a, b):
        product = dot(a, b, TN)
        state = jnp.where(state_low, product[:DH], product[DH:])
        for h in range(CORES):
            own[at(h, p), :] = state[h * HALF:(h + 1) * HALF]

    positions = (seq * GROUP + iota((GROUP, PAIR), 0)).astype(F32)
    factor = 1.0 / jnp.sqrt(DH * (positions + 1.0))

    def scaled(a):
        return (a.astype(F32) * factor).astype(BF16)

    def to_sibling(own, sib, need, rest):
        theirs, mine = aligned(1 - core, half), aligned(core, half)
        send(own.at[theirs], sib.at[theirs], need, sibling)
        send(own.at[mine], sib.at[mine], rest, sibling)

    def to_owners(own, sib, chip, which, places):
        mine = aligned(core, half)
        arrived(sib.at[mine], which)
        chip[...] = (own[mine, :] + sib[mine, :]).astype(BF16)
        for i, place in enumerate(places):
            piece = chip.at[pl.ds(i * chunk, chunk)]

            @pl.when(z != place)
            def _(piece=piece, place=place):
                send(piece, line.at[aligned(z, chunk)], OUT, device(x, place, core))

            @pl.when(z == place)
            def _(i=i, place=place):
                line[place * chunk:(place + 1) * chunk, :] = chip[i * chunk:(i + 1) * chunk, :]

    def sum_chunk(place, backward):
        arrived(line.at[pl.ds(0, (zs - 1) * chunk)], OUT)
        total = None
        for step in range(zs):
            zz = zs - 1 - step if backward else step
            piece = line[zz * chunk:(zz + 1) * chunk, :].astype(F32)
            part[zz * chunk:(zz + 1) * chunk, :] = jnp.zeros_like(piece) if total is None else total
            total = piece if total is None else total + piece
        totals[aligned(x, chunk), :] = total.astype(BF16)
        for xx in range(xs):
            def pass_on(xx=xx):
                send(totals.at[aligned(x, chunk)], totals.at[aligned(x, chunk)], TOT, device(xx, place, core))

            pl.when(xx < x if backward else xx > x)(pass_on)
    def return_chunk(scan, which, i, place, backward):
        waits = (lambda xx: xs - 1 - xx) if backward else (lambda xx: xx)
        for xx in range(xs):
            if waits(xx):

                @pl.when(x == xx)
                def _(n=waits(xx)):
                    arrived(totals.at[pl.ds(0, n * chunk)], TOT)

        base = jnp.zeros((chunk, PAIR), F32)
        for xx in range(xs):
            counts = xx > x if backward else xx < x
            base = base + jnp.where(counts, totals[xx * chunk:(xx + 1) * chunk, :].astype(F32), 0.0)
        home = pl.ds(pl.multiple_of(core * half + i * chunk, chunk), chunk)
        for zz in back_order:
            line_out[zz * chunk:(zz + 1) * chunk, :] = (part[zz * chunk:(zz + 1) * chunk, :] + base).astype(BF16)
            piece = line_out.at[pl.ds(zz * chunk, chunk)]
            if zz == place:
                send(piece, scan.at[home], which, sibling)
                scan[home, :] = line_out[zz * chunk:(zz + 1) * chunk, :]
            else:
                for cc in range(CORES):
                    send(piece, scan.at[home], which, device(x, zz, cc))

    def sum_one(places, backward):
        for place in places:
            pl.when(z == place)(functools.partial(sum_chunk, place, backward))

    def return_one(scan, which, places, backward):
        for i, place in enumerate(places):
            pl.when(z == place)(functools.partial(return_chunk, scan, which, i, place, backward))

    def came_back(scan, which, places):
        mine = among(z, places)

        @pl.when(mine)
        def _():
            arrived(scan.at[pl.ds(0, CORES * half - chunk)], which)

        @pl.when(jnp.logical_not(mine))
        def _():
            arrived(scan, which)

    def state_of(scan, sib, weight, p):
        rows = [scan[at(h, p), :].astype(F32) + weight * sib[at(h, p), :] for h in range(CORES)]
        return diagonal(jnp.concatenate(rows, axis=0)).astype(BF16)

    loads[0].wait()
    pl.semaphore_wait(barrier, greeted)
    for d in range(1, ys):
        to = (y + d) % ys
        send(g_in.at[:, aligned(to, width)], g.at[aligned(y, rows_y)], G, (seq, to))
    loads[1].wait()
    loads[2].wait()
    for p in range(pairs):
        pair_state(own_f, p, k[:, columns(p)], v[:, columns(p)])
    to_sibling(own_f, sib_f, CF, CF2)
    g[aligned(y, rows_y), :] = g_in[:, aligned(y, width)]

    causal = iota((2 * GROUP, GROUP), 0) % GROUP >= iota((2 * GROUP, GROUP), 1)
    causal_t = iota((GROUP, 2 * GROUP), 1) % GROUP >= iota((GROUP, 2 * GROUP), 0)
    to_owners(own_f, sib_f, chip_f, CF, forward_at)

    loads[3].wait()
    for p in range(pairs):
        c = columns(p)
        scores = jnp.where(causal, dot(split(scaled(q[:, c])), k[:, c], NT), 0.0).astype(BF16)
        attn_l[:, c] = dot(beside(scores), split(v[:, c]))

    arrived(g.at[pl.ds(0, (ys - 1) * rows_y)], G)
    for p in range(pairs):
        pair_state(own_r, p, q[:, columns(p)], scaled(g[:, columns(p)]))
    to_sibling(own_r, sib_r, CR, CR2)
    to_owners(own_r, sib_r, chip_r, CR, backward_at)

    for p in range(pairs):
        c = columns(p)
        g_two, q_two = split(scaled(g[:, c])), split(q[:, c])
        grad_scores = jnp.where(causal, dot(g_two, v[:, c], NT), 0.0).astype(BF16)
        gq_l[:, c] = dot(beside(grad_scores), split(k[:, c]))
        grad_scores_t = jnp.where(causal_t, dot(v[:, c], g_two, NT), 0.0).astype(BF16)
        gk_l[:, c] = dot(grad_scores_t, q_two)
        plain_t = jnp.where(causal_t, dot(k[:, c], q_two, NT), 0.0).astype(BF16)
        gv_l[:, c] = dot(plain_t, g_two)

    sum_one(forward_at, False)
    return_one(scan_f, BF, forward_at, False)
    sum_one(backward_at, True)

    after = core.astype(F32)
    arrived(sib_f.at[aligned(1 - core, half)], CF2)
    came_back(scan_f, BF, forward_at)
    for p in range(pairs):
        c = columns(p)
        state = state_of(scan_f, sib_f, after, p)
        attn_s[:, c] = (attn_l[:, c] + dot(scaled(q[:, c]), state)).astype(BF16)
    for d in range(1, ys):
        to = (y + d) % ys
        send(attn_s.at[aligned(to, rows_y)], attn_r.at[:, aligned(y, width)], AT, (seq, to))
    attn_r[:, aligned(y, width)] = attn_s[aligned(y, rows_y), :]
    return_one(scan_r, BR, backward_at, True)
    for p in range(pairs):
        c = columns(p)
        state = state_of(scan_f, sib_f, after, p)
        gq_s[:, c] = (gq_l[:, c] + dot(scaled(g[:, c]), state, NT)).astype(BF16)

    arrived(sib_r.at[aligned(1 - core, half)], CR2)
    came_back(scan_r, BR, backward_at)
    for p in range(pairs):
        c = columns(p)
        state = state_of(scan_r, sib_r, 1.0 - after, p)
        gk_s[:, c] = (gk_l[:, c] + dot(v[:, c], state, NT)).astype(BF16)
        gv_s[:, c] = (gv_l[:, c] + dot(k[:, c], state)).astype(BF16)

    arrived(attn_r.at[:, pl.ds(0, (ys - 1) * width)], AT)

    sent(g.at[pl.ds(0, (ys - 1) * rows_y)], G)
    for which in (CF, CF2, CR, CR2):
        sent(own_f.at[pl.ds(0, half)], which)
    sent(attn_r.at[:, pl.ds(0, (ys - 1) * width)], AT)

    @pl.when(jnp.logical_not(owner))
    def _():
        sent(chip_f, OUT)
        sent(chip_r, OUT)

    @pl.when(owner)
    def _():
        sent(chip_f, OUT)
        sent(chip_r.at[pl.ds(0, half - chunk)], OUT)

    for places, which in ((forward_at, BF), (backward_at, BR)):

        @pl.when(among(z, places))
        def _(which=which):
            sent(line_out, which)
            sent(line_out.at[pl.ds(0, (zs - 1) * chunk)], which)
            for xx in range(xs):
                n = xx if which == BR else xs - 1 - xx
                if n:
                    pl.when(x == xx)(functools.partial(sent, totals.at[pl.ds(0, n * chunk)], TOT))


def write_out(*refs):
    copies = [pltpu.make_async_copy(refs[i], refs[4 + i], refs[8].at[i]) for i in range(4)]
    for copy in copies:
        copy.start()
    for copy in copies:
        copy.wait()


def shards(xs, zs, ys, forward_at, backward_at, back_order, query_rot, key_rot, value_rot, grad_out):
    tok, width = query_rot.shape
    half = width // PAIR * HALF
    chunk = half // len(forward_at)
    block = pltpu.VMEM((tok, width), BF16)
    wide = pltpu.VMEM((tok, width), F32)
    state = pltpu.VMEM((CORES * half, PAIR), F32)
    chip = pltpu.VMEM((half, PAIR), BF16)
    line = pltpu.VMEM((zs * chunk, PAIR), BF16)
    scan = pltpu.VMEM((CORES * half, PAIR), BF16)
    operands = [pltpu.with_memory_space_constraint(a, pltpu.HBM) for a in (query_rot, key_rot, value_rot, grad_out)]
    results = pl.pallas_call(
        functools.partial(kernel, xs, zs, ys, forward_at, backward_at, back_order),
        out_shape=(pltpu.VMEM(grad_out.shape, BF16), block, block, block),
        in_specs=[pl.BlockSpec(memory_space=pltpu.HBM)] * 4,
        out_specs=(pl.BlockSpec(memory_space=pltpu.VMEM),) * 4,
        scratch_shapes=[
            block, block, block, pltpu.VMEM(grad_out.shape, BF16), block,
            state, state, state, state,
            chip, chip,
            line, pltpu.VMEM((zs * chunk, PAIR), F32), line,
            pltpu.VMEM((xs * chunk, PAIR), BF16),
            scan, scan,
            wide, wide, wide, wide,
            block,
            pltpu.SemaphoreType.DMA((4,)),
            pltpu.SemaphoreType.DMA((10,)),
            pltpu.SemaphoreType.DMA((10,)),
        ],
        compiler_params=pltpu.CompilerParams(
            collective_id=0, has_side_effects=True, vmem_limit_bytes=32 * 2**20
        ),
    )(*operands)
    return pl.pallas_call(
        write_out,
        out_shape=tuple(jax.ShapeDtypeStruct(a.shape, a.dtype) for a in results),
        in_specs=[pl.BlockSpec(memory_space=pltpu.VMEM)] * 4,
        out_specs=(pl.BlockSpec(memory_space=pltpu.HBM),) * 4,
        scratch_shapes=[pltpu.SemaphoreType.DMA((4,))],
    )(*[pltpu.with_memory_space_constraint(a, pltpu.VMEM) for a in results])


def solution(mesh, xs=XS, zs=ZS, forward_at=FORWARD_AT, backward_at=BACKWARD_AT, back_order=BACK_ORDER):
    in_specs = (P("seq", "head"), P("seq", "head"), P("seq", "head"), P(("seq", "head"), None))
    out_specs = (P(("seq", "head"), None), P("seq", "head"), P("seq", "head"), P("seq", "head"))
    return jax.shard_map(
        functools.partial(shards, xs, zs, mesh.shape["head"], forward_at, backward_at, back_order),
        mesh=mesh, in_specs=in_specs, out_specs=out_specs, check_vma=False,
    )
```

```python
import functools

import jax
import jax.numpy as jnp
from jax import lax
from jax.experimental import pallas as pl
from jax.experimental.pallas import tpu as pltpu
from jax.sharding import PartitionSpec as P

DH = 64
GROUP = 128
XS = 4
ZS = 16
CORES = 2
PAIR = 2 * DH
HALF = DH // CORES
FORWARD_AT = (12, 14, 0, 2)
BACKWARD_AT = (13, 15, 1, 3)
BACK_ORDER = (0, 1, 2, 15, 3, 14, 4, 13, 5, 12, 6, 11, 7, 10, 8, 9)
MESH = pl.DeviceIdType.MESH
F32 = jnp.float32
BF16 = jnp.bfloat16

NN = (((1,), (0,)), ((), ()))
NT = (((1,), (1,)), ((), ()))
TN = (((0,), (0,)), ((), ()))
G, CF, CR, CF2, CR2, OUT, TOT, BF, BR, AT = range(10)


def dot(a, b, dims=NN):
    return lax.dot_general(a, b, dims, preferred_element_type=F32)


def iota(shape, dim):
    return lax.broadcasted_iota(jnp.int32, shape, dim)


def kernel(
    xs, zs, ys, forward_at, backward_at, back_order,
    q_hbm, k_hbm, v_hbm, g_hbm,
    attn_r, gq_s, gk_s, gv_s,
    q, k, v, g_in, g,
    own_f, own_r, sib_f, sib_r,
    chip_f, chip_r,
    line, part, line_out,
    totals,
    scan_f, scan_r,
    attn_l, gq_l, gk_l, gv_l,
    attn_s,
    in_sem, send_sem, recv_sem,
):
    width = q.shape[1]
    pairs = width // PAIR
    half = pairs * HALF
    chunk = half // len(forward_at)
    rows_y = GROUP // ys

    seq = lax.axis_index("seq")
    y = lax.axis_index("head")
    x = seq // (zs * CORES)
    z = (seq // CORES) % zs
    core = seq % CORES

    def device(xx, zz, cc):
        return ((xx * zs + zz) * CORES + cc, y)

    def among(zz, places):
        found = zz == places[0]
        for place in places[1:]:
            found = jnp.logical_or(found, zz == place)
        return found

    def aligned(i, n):
        return pl.ds(pl.multiple_of(i * n, n), n)

    def send(src, dst, which, to):
        pltpu.make_async_remote_copy(
            src_ref=src, dst_ref=dst, send_sem=send_sem.at[which], recv_sem=recv_sem.at[which],
            device_id=to, device_id_type=MESH,
        ).start()

    def arrived(ref, which):
        pltpu.make_async_copy(ref, ref, recv_sem.at[which]).wait()

    def sent(ref, which):
        pltpu.make_async_copy(ref, ref, send_sem.at[which]).wait()

    barrier = pltpu.get_barrier_semaphore()
    both = forward_at + backward_at
    owner = among(z, both)
    sibling = device(x, z, 1 - core)

    def greet(to):
        pl.semaphore_signal(barrier, inc=1, device_id=to, device_id_type=MESH)

    for d in range(1, ys):
        greet((seq, (y + d) % ys))
    for d in range(1, xs):
        greet(device((x + d) % xs, z, core))
    greet(sibling)
    for zz in range(zs):
        for cc in range(CORES):
            meet = jnp.logical_and(True if zz in both else owner, z != zz)
            pl.when(meet)(functools.partial(greet, device(x, zz, cc)))
    greeted = ys - 1 + xs - 1 + 1 + CORES * jnp.where(owner, zs - 1, len(both))

    loads = [
        pltpu.make_async_copy(src, dst, in_sem.at[i])
        for i, (src, dst) in enumerate(
            (
                (g_hbm, g_in), (k_hbm, k), (v_hbm, v), (q_hbm, q),
            )
        )
    ]
    for load in loads:
        load.start()

    lane_low = iota((GROUP, PAIR), 1) < DH
    state_low = iota((DH, PAIR), 1) < DH

    def split(a):
        return jnp.concatenate([jnp.where(lane_low, a, 0), jnp.where(lane_low, 0, a)], axis=0)

    def beside(a):
        return jnp.concatenate([a[:GROUP], a[GROUP:]], axis=1)

    def diagonal(s):
        return jnp.concatenate([jnp.where(state_low, s, 0), jnp.where(state_low, 0, s)], axis=0)

    def columns(p):
        return slice(p * PAIR, (p + 1) * PAIR)

    def at(h, p):
        return slice(h * half + p * HALF, h * half + (p + 1) * HALF)

    def pair_state(own, p, a, b):
        product = dot(a, b, TN)
        state = jnp.where(state_low, product[:DH], product[DH:])
        for h in range(CORES):
            own[at(h, p), :] = state[h * HALF:(h + 1) * HALF]

    positions = (seq * GROUP + iota((GROUP, PAIR), 0)).astype(F32)
    factor = 1.0 / jnp.sqrt(DH * (positions + 1.0))

    def scaled(a):
        return (a.astype(F32) * factor).astype(BF16)

    def to_sibling(own, sib, need, rest):
        theirs, mine = aligned(1 - core, half), aligned(core, half)
        send(own.at[theirs], sib.at[theirs], need, sibling)
        send(own.at[mine], sib.at[mine], rest, sibling)

    def to_owners(own, sib, chip, which, places):
        mine = aligned(core, half)
        arrived(sib.at[mine], which)
        chip[...] = (own[mine, :] + sib[mine, :]).astype(BF16)
        for i, place in enumerate(places):
            piece = chip.at[pl.ds(i * chunk, chunk)]

            @pl.when(z != place)
            def _(piece=piece, place=place):
                send(piece, line.at[aligned(z, chunk)], OUT, device(x, place, core))

            @pl.when(z == place)
            def _(i=i, place=place):
                line[place * chunk:(place + 1) * chunk, :] = chip[i * chunk:(i + 1) * chunk, :]

    def sum_chunk(place, backward):
        arrived(line.at[pl.ds(0, (zs - 1) * chunk)], OUT)
        total = None
        for step in range(zs):
            zz = zs - 1 - step if backward else step
            piece = line[zz * chunk:(zz + 1) * chunk, :].astype(F32)
            part[zz * chunk:(zz + 1) * chunk, :] = jnp.zeros_like(piece) if total is None else total
            total = piece if total is None else total + piece
        totals[aligned(x, chunk), :] = total
        for xx in range(xs):
            def pass_on(xx=xx):
                send(totals.at[aligned(x, chunk)], totals.at[aligned(x, chunk)], TOT, device(xx, place, core))

            pl.when(xx < x if backward else xx > x)(pass_on)
    def return_chunk(scan, which, i, place, backward):
        waits = (lambda xx: xs - 1 - xx) if backward else (lambda xx: xx)
        for xx in range(xs):
            if waits(xx):

                @pl.when(x == xx)
                def _(n=waits(xx)):
                    arrived(totals.at[pl.ds(0, n * chunk)], TOT)

        base = jnp.zeros((chunk, PAIR), F32)
        for xx in range(xs):
            counts = xx > x if backward else xx < x
            base = base + jnp.where(counts, totals[xx * chunk:(xx + 1) * chunk, :], 0.0)
        home = pl.ds(pl.multiple_of(core * half + i * chunk, chunk), chunk)
        for zz in back_order:
            line_out[zz * chunk:(zz + 1) * chunk, :] = (part[zz * chunk:(zz + 1) * chunk, :] + base).astype(BF16)
            piece = line_out.at[pl.ds(zz * chunk, chunk)]
            if zz == place:
                send(piece, scan.at[home], which, sibling)
                scan[home, :] = line_out[zz * chunk:(zz + 1) * chunk, :]
            else:
                for cc in range(CORES):
                    send(piece, scan.at[home], which, device(x, zz, cc))

    def sum_one(places, backward):
        for place in places:
            pl.when(z == place)(functools.partial(sum_chunk, place, backward))

    def return_one(scan, which, places, backward):
        for i, place in enumerate(places):
            pl.when(z == place)(functools.partial(return_chunk, scan, which, i, place, backward))

    def came_back(scan, which, places):
        mine = among(z, places)

        @pl.when(mine)
        def _():
            arrived(scan.at[pl.ds(0, CORES * half - chunk)], which)

        @pl.when(jnp.logical_not(mine))
        def _():
            arrived(scan, which)

    def state_of(scan, sib, weight, p):
        rows = [scan[at(h, p), :].astype(F32) + weight * sib[at(h, p), :] for h in range(CORES)]
        return diagonal(jnp.concatenate(rows, axis=0)).astype(BF16)

    loads[0].wait()
    pl.semaphore_wait(barrier, greeted)
    for d in range(1, ys):
        to = (y + d) % ys
        send(g_in.at[:, aligned(to, width)], g.at[aligned(y, rows_y)], G, (seq, to))
    loads[1].wait()
    loads[2].wait()
    for p in range(pairs):
        pair_state(own_f, p, k[:, columns(p)], v[:, columns(p)])
    to_sibling(own_f, sib_f, CF, CF2)
    g[aligned(y, rows_y), :] = g_in[:, aligned(y, width)]

    causal = iota((2 * GROUP, GROUP), 0) % GROUP >= iota((2 * GROUP, GROUP), 1)
    causal_t = iota((GROUP, 2 * GROUP), 1) % GROUP >= iota((GROUP, 2 * GROUP), 0)
    to_owners(own_f, sib_f, chip_f, CF, forward_at)

    loads[3].wait()
    for p in range(pairs):
        c = columns(p)
        scores = jnp.where(causal, dot(split(scaled(q[:, c])), k[:, c], NT), 0.0).astype(BF16)
        attn_l[:, c] = dot(beside(scores), split(v[:, c]))

    arrived(g.at[pl.ds(0, (ys - 1) * rows_y)], G)
    for p in range(pairs):
        pair_state(own_r, p, q[:, columns(p)], scaled(g[:, columns(p)]))
    to_sibling(own_r, sib_r, CR, CR2)
    to_owners(own_r, sib_r, chip_r, CR, backward_at)

    for p in range(pairs):
        c = columns(p)
        g_two, q_two = split(scaled(g[:, c])), split(q[:, c])
        grad_scores = jnp.where(causal, dot(g_two, v[:, c], NT), 0.0).astype(BF16)
        gq_l[:, c] = dot(beside(grad_scores), split(k[:, c]))
        grad_scores_t = jnp.where(causal_t, dot(v[:, c], g_two, NT), 0.0).astype(BF16)
        gk_l[:, c] = dot(grad_scores_t, q_two)
        plain_t = jnp.where(causal_t, dot(k[:, c], q_two, NT), 0.0).astype(BF16)
        gv_l[:, c] = dot(plain_t, g_two)

    sum_one(forward_at, False)
    return_one(scan_f, BF, forward_at, False)
    sum_one(backward_at, True)

    after = core.astype(F32)
    arrived(sib_f.at[aligned(1 - core, half)], CF2)
    came_back(scan_f, BF, forward_at)
    for p in range(pairs):
        c = columns(p)
        state = state_of(scan_f, sib_f, after, p)
        attn_s[:, c] = (attn_l[:, c] + dot(scaled(q[:, c]), state)).astype(BF16)
    for d in range(1, ys):
        to = (y + d) % ys
        send(attn_s.at[aligned(to, rows_y)], attn_r.at[:, aligned(y, width)], AT, (seq, to))
    attn_r[:, aligned(y, width)] = attn_s[aligned(y, rows_y), :]
    return_one(scan_r, BR, backward_at, True)
    for p in range(pairs):
        c = columns(p)
        state = state_of(scan_f, sib_f, after, p)
        gq_s[:, c] = (gq_l[:, c] + dot(scaled(g[:, c]), state, NT)).astype(BF16)

    arrived(sib_r.at[aligned(1 - core, half)], CR2)
    came_back(scan_r, BR, backward_at)
    for p in range(pairs):
        c = columns(p)
        state = state_of(scan_r, sib_r, 1.0 - after, p)
        gk_s[:, c] = (gk_l[:, c] + dot(v[:, c], state, NT)).astype(BF16)
        gv_s[:, c] = (gv_l[:, c] + dot(k[:, c], state)).astype(BF16)

    arrived(attn_r.at[:, pl.ds(0, (ys - 1) * width)], AT)

    sent(g.at[pl.ds(0, (ys - 1) * rows_y)], G)
    for which in (CF, CF2, CR, CR2):
        sent(own_f.at[pl.ds(0, half)], which)
    sent(attn_r.at[:, pl.ds(0, (ys - 1) * width)], AT)

    @pl.when(jnp.logical_not(owner))
    def _():
        sent(chip_f, OUT)
        sent(chip_r, OUT)

    @pl.when(owner)
    def _():
        sent(chip_f, OUT)
        sent(chip_r.at[pl.ds(0, half - chunk)], OUT)

    for places, which in ((forward_at, BF), (backward_at, BR)):

        @pl.when(among(z, places))
        def _(which=which):
            sent(line_out, which)
            sent(line_out.at[pl.ds(0, (zs - 1) * chunk)], which)
            for xx in range(xs):
                n = xx if which == BR else xs - 1 - xx
                if n:
                    pl.when(x == xx)(functools.partial(sent, totals.at[pl.ds(0, n * chunk)], TOT))


def write_out(*refs):
    copies = [pltpu.make_async_copy(refs[i], refs[4 + i], refs[8].at[i]) for i in range(4)]
    for copy in copies:
        copy.start()
    for copy in copies:
        copy.wait()


def shards(xs, zs, ys, forward_at, backward_at, back_order, query_rot, key_rot, value_rot, grad_out):
    tok, width = query_rot.shape
    half = width // PAIR * HALF
    chunk = half // len(forward_at)
    block = pltpu.VMEM((tok, width), BF16)
    wide = pltpu.VMEM((tok, width), F32)
    state = pltpu.VMEM((CORES * half, PAIR), F32)
    chip = pltpu.VMEM((half, PAIR), BF16)
    line = pltpu.VMEM((zs * chunk, PAIR), BF16)
    scan = pltpu.VMEM((CORES * half, PAIR), BF16)
    operands = [pltpu.with_memory_space_constraint(a, pltpu.HBM) for a in (query_rot, key_rot, value_rot, grad_out)]
    results = pl.pallas_call(
        functools.partial(kernel, xs, zs, ys, forward_at, backward_at, back_order),
        out_shape=(pltpu.VMEM(grad_out.shape, BF16), block, block, block),
        in_specs=[pl.BlockSpec(memory_space=pltpu.HBM)] * 4,
        out_specs=(pl.BlockSpec(memory_space=pltpu.VMEM),) * 4,
        scratch_shapes=[
            block, block, block, pltpu.VMEM(grad_out.shape, BF16), block,
            state, state, state, state,
            chip, chip,
            line, pltpu.VMEM((zs * chunk, PAIR), F32), line,
            pltpu.VMEM((xs * chunk, PAIR), F32),
            scan, scan,
            wide, wide, wide, wide,
            block,
            pltpu.SemaphoreType.DMA((4,)),
            pltpu.SemaphoreType.DMA((10,)),
            pltpu.SemaphoreType.DMA((10,)),
        ],
        compiler_params=pltpu.CompilerParams(
            collective_id=0, has_side_effects=True, vmem_limit_bytes=32 * 2**20
        ),
    )(*operands)
    return pl.pallas_call(
        write_out,
        out_shape=tuple(jax.ShapeDtypeStruct(a.shape, a.dtype) for a in results),
        in_specs=[pl.BlockSpec(memory_space=pltpu.VMEM)] * 4,
        out_specs=(pl.BlockSpec(memory_space=pltpu.HBM),) * 4,
        scratch_shapes=[pltpu.SemaphoreType.DMA((4,))],
    )(*[pltpu.with_memory_space_constraint(a, pltpu.VMEM) for a in results])


def solution(mesh, xs=XS, zs=ZS, forward_at=FORWARD_AT, backward_at=BACKWARD_AT, back_order=BACK_ORDER):
    in_specs = (P("seq", "head"), P("seq", "head"), P("seq", "head"), P(("seq", "head"), None))
    out_specs = (P(("seq", "head"), None), P("seq", "head"), P("seq", "head"), P("seq", "head"))
    return jax.shard_map(
        functools.partial(shards, xs, zs, mesh.shape["head"], forward_at, backward_at, back_order),
        mesh=mesh, in_specs=in_specs, out_specs=out_specs, check_vma=False,
    )
```

```python
import functools

import jax
import jax.numpy as jnp
from jax import lax
from jax.experimental import pallas as pl
from jax.experimental.pallas import tpu as pltpu
from jax.sharding import PartitionSpec as P

DH = 64
GROUP = 128
XS = 4
ZS = 16
CORES = 2
PAIR = 2 * DH
HALF = DH // CORES
FORWARD_AT = (12, 14, 0, 2)
BACKWARD_AT = (13, 15, 1, 3)
BACK_ORDER = (0, 1, 2, 15, 3, 14, 4, 13, 5, 12, 6, 11, 7, 10, 8, 9)
MESH = pl.DeviceIdType.MESH
F32 = jnp.float32
BF16 = jnp.bfloat16

NN = (((1,), (0,)), ((), ()))
NT = (((1,), (1,)), ((), ()))
TN = (((0,), (0,)), ((), ()))
G, CF, CR, CF2, CR2, OUT, TOT, BF, BR, AT = range(10)


def dot(a, b, dims=NN):
    return lax.dot_general(a, b, dims, preferred_element_type=F32)


def iota(shape, dim):
    return lax.broadcasted_iota(jnp.int32, shape, dim)


def kernel(
    xs, zs, ys, forward_at, backward_at, back_order,
    q_hbm, k_hbm, v_hbm, g_hbm,
    attn_r, gq_s, gk_s, gv_s,
    q, k, v, g_in, g,
    own_f, own_r, sib_f, sib_r,
    chip_f, chip_r,
    line, part, line_out,
    totals,
    scan_f, scan_r,
    attn_l, gq_l, gk_l, gv_l,
    attn_s,
    in_sem, send_sem, recv_sem,
):
    width = q.shape[1]
    pairs = width // PAIR
    half = pairs * HALF
    chunk = half // len(forward_at)
    rows_y = GROUP // ys

    seq = lax.axis_index("seq")
    y = lax.axis_index("head")
    x = seq // (zs * CORES)
    z = (seq // CORES) % zs
    core = seq % CORES

    def device(xx, zz, cc):
        return ((xx * zs + zz) * CORES + cc, y)

    def among(zz, places):
        found = zz == places[0]
        for place in places[1:]:
            found = jnp.logical_or(found, zz == place)
        return found

    def aligned(i, n):
        return pl.ds(pl.multiple_of(i * n, n), n)

    def send(src, dst, which, to):
        pltpu.make_async_remote_copy(
            src_ref=src, dst_ref=dst, send_sem=send_sem.at[which], recv_sem=recv_sem.at[which],
            device_id=to, device_id_type=MESH,
        ).start()

    def arrived(ref, which):
        pltpu.make_async_copy(ref, ref, recv_sem.at[which]).wait()

    def sent(ref, which):
        pltpu.make_async_copy(ref, ref, send_sem.at[which]).wait()

    barrier = pltpu.get_barrier_semaphore()
    both = forward_at + backward_at
    owner = among(z, both)
    sibling = device(x, z, 1 - core)

    def greet(to):
        pl.semaphore_signal(barrier, inc=1, device_id=to, device_id_type=MESH)

    for d in range(1, ys):
        greet((seq, (y + d) % ys))
    for d in range(1, xs):
        greet(device((x + d) % xs, z, core))
    greet(sibling)
    for zz in range(zs):
        for cc in range(CORES):
            meet = jnp.logical_and(True if zz in both else owner, z != zz)
            pl.when(meet)(functools.partial(greet, device(x, zz, cc)))
    greeted = ys - 1 + xs - 1 + 1 + CORES * jnp.where(owner, zs - 1, len(both))

    loads = [
        pltpu.make_async_copy(src, dst, in_sem.at[i])
        for i, (src, dst) in enumerate(
            (
                (g_hbm, g_in), (k_hbm, k), (v_hbm, v), (q_hbm, q),
            )
        )
    ]
    for load in loads:
        load.start()

    lane_low = iota((GROUP, PAIR), 1) < DH
    state_low = iota((DH, PAIR), 1) < DH

    def split(a):
        return jnp.concatenate([jnp.where(lane_low, a, 0), jnp.where(lane_low, 0, a)], axis=0)

    def beside(a):
        return jnp.concatenate([a[:GROUP], a[GROUP:]], axis=1)

    def diagonal(s):
        return jnp.concatenate([jnp.where(state_low, s, 0), jnp.where(state_low, 0, s)], axis=0)

    def columns(p):
        return slice(p * PAIR, (p + 1) * PAIR)

    def at(h, p):
        return slice(h * half + p * HALF, h * half + (p + 1) * HALF)

    def pair_state(own, p, a, b):
        product = dot(a, b, TN)
        state = jnp.where(state_low, product[:DH], product[DH:])
        for h in range(CORES):
            own[at(h, p), :] = state[h * HALF:(h + 1) * HALF]

    positions = (seq * GROUP + iota((GROUP, PAIR), 0)).astype(F32)
    factor = 1.0 / jnp.sqrt(DH * (positions + 1.0))

    def scaled(a):
        return (a.astype(F32) * factor).astype(BF16)

    def to_sibling(own, sib, need, rest):
        theirs, mine = aligned(1 - core, half), aligned(core, half)
        send(own.at[theirs], sib.at[theirs], need, sibling)
        send(own.at[mine], sib.at[mine], rest, sibling)

    def to_owners(own, sib, chip, which, places):
        mine = aligned(core, half)
        arrived(sib.at[mine], which)
        chip[...] = (own[mine, :] + sib[mine, :]).astype(BF16)
        for i, place in enumerate(places):
            piece = chip.at[pl.ds(i * chunk, chunk)]

            @pl.when(z != place)
            def _(piece=piece, place=place):
                send(piece, line.at[aligned(z, chunk)], OUT, device(x, place, core))

            @pl.when(z == place)
            def _(i=i, place=place):
                line[place * chunk:(place + 1) * chunk, :] = chip[i * chunk:(i + 1) * chunk, :]

    def sum_chunk(place, backward):
        arrived(line.at[pl.ds(0, (zs - 1) * chunk)], OUT)
        total = None
        for step in range(zs):
            zz = zs - 1 - step if backward else step
            piece = line[zz * chunk:(zz + 1) * chunk, :].astype(F32)
            part[zz * chunk:(zz + 1) * chunk, :] = jnp.zeros_like(piece) if total is None else total
            total = piece if total is None else total + piece
        totals[aligned(x, chunk), :] = total
        for xx in range(xs):
            def pass_on(xx=xx):
                send(totals.at[aligned(x, chunk)], totals.at[aligned(x, chunk)], TOT, device(xx, place, core))

            pl.when(xx < x if backward else xx > x)(pass_on)
    def return_chunk(scan, which, i, place, backward):
        waits = (lambda xx: xs - 1 - xx) if backward else (lambda xx: xx)
        for xx in range(xs):
            if waits(xx):

                @pl.when(x == xx)
                def _(n=waits(xx)):
                    arrived(totals.at[pl.ds(0, n * chunk)], TOT)

        base = jnp.zeros((chunk, PAIR), F32)
        for xx in range(xs):
            counts = xx > x if backward else xx < x
            base = base + jnp.where(counts, totals[xx * chunk:(xx + 1) * chunk, :], 0.0)
        home = pl.ds(pl.multiple_of(core * half + i * chunk, chunk), chunk)
        for zz in back_order:
            line_out[zz * chunk:(zz + 1) * chunk, :] = (part[zz * chunk:(zz + 1) * chunk, :] + base).astype(BF16)
            piece = line_out.at[pl.ds(zz * chunk, chunk)]
            if zz == place:
                send(piece, scan.at[home], which, sibling)
                scan[home, :] = line_out[zz * chunk:(zz + 1) * chunk, :]
            else:
                for cc in range(CORES):
                    send(piece, scan.at[home], which, device(x, zz, cc))

    def sum_one(places, backward):
        for place in places:
            pl.when(z == place)(functools.partial(sum_chunk, place, backward))

    def return_one(scan, which, places, backward):
        for i, place in enumerate(places):
            pl.when(z == place)(functools.partial(return_chunk, scan, which, i, place, backward))

    def came_back(scan, which, places):
        mine = among(z, places)

        @pl.when(mine)
        def _():
            arrived(scan.at[pl.ds(0, CORES * half - chunk)], which)

        @pl.when(jnp.logical_not(mine))
        def _():
            arrived(scan, which)

    def state_of(scan, sib, weight, p):
        rows = [scan[at(h, p), :].astype(F32) + weight * sib[at(h, p), :] for h in range(CORES)]
        return diagonal(jnp.concatenate(rows, axis=0)).astype(BF16)

    loads[0].wait()
    pl.semaphore_wait(barrier, greeted)
    for d in range(1, ys):
        to = (y + d) % ys
        send(g_in.at[:, aligned(to, width)], g.at[aligned(y, rows_y)], G, (seq, to))
    loads[1].wait()
    loads[2].wait()
    for p in range(pairs):
        pair_state(own_f, p, k[:, columns(p)], v[:, columns(p)])
    to_sibling(own_f, sib_f, CF, CF2)
    g[aligned(y, rows_y), :] = g_in[:, aligned(y, width)]

    causal = iota((2 * GROUP, GROUP), 0) % GROUP >= iota((2 * GROUP, GROUP), 1)
    causal_t = iota((GROUP, 2 * GROUP), 1) % GROUP >= iota((GROUP, 2 * GROUP), 0)
    to_owners(own_f, sib_f, chip_f, CF, forward_at)

    loads[3].wait()
    for p in range(pairs):
        c = columns(p)
        scores = jnp.where(causal, dot(split(scaled(q[:, c])), k[:, c], NT), 0.0).astype(BF16)
        attn_l[:, c] = dot(beside(scores), split(v[:, c]))

    arrived(g.at[pl.ds(0, (ys - 1) * rows_y)], G)
    for p in range(pairs):
        pair_state(own_r, p, q[:, columns(p)], scaled(g[:, columns(p)]))
    to_sibling(own_r, sib_r, CR, CR2)
    to_owners(own_r, sib_r, chip_r, CR, backward_at)

    for p in range(pairs):
        c = columns(p)
        g_two, q_two = split(scaled(g[:, c])), split(q[:, c])
        grad_scores = jnp.where(causal, dot(g_two, v[:, c], NT), 0.0).astype(BF16)
        gq_l[:, c] = dot(beside(grad_scores), split(k[:, c]))
        grad_scores_t = jnp.where(causal_t, dot(v[:, c], g_two, NT), 0.0).astype(BF16)
        gk_l[:, c] = dot(grad_scores_t, q_two)
        plain_t = jnp.where(causal_t, dot(k[:, c], q_two, NT), 0.0).astype(BF16)
        gv_l[:, c] = dot(plain_t, g_two)

    sum_one(forward_at, False)
    return_one(scan_f, BF, forward_at, False)
    sum_one(backward_at, True)

    after = core.astype(F32)
    arrived(sib_f.at[aligned(1 - core, half)], CF2)
    came_back(scan_f, BF, forward_at)
    for p in range(pairs):
        c = columns(p)
        state = state_of(scan_f, sib_f, after, p)
        attn_s[:, c] = (attn_l[:, c] + dot(scaled(q[:, c]), state)).astype(BF16)
        if p % 2:
            first = (p - 1) * PAIR
            there = pl.ds(pl.multiple_of(y * width + first, PAIR), 2 * PAIR)
            for d in range(1, ys):
                to = (y + d) % ys
                send(attn_s.at[aligned(to, rows_y), pl.ds(first, 2 * PAIR)], attn_r.at[:, there], AT, (seq, to))
    attn_r[:, aligned(y, width)] = attn_s[aligned(y, rows_y), :]
    return_one(scan_r, BR, backward_at, True)
    for p in range(pairs):
        c = columns(p)
        state = state_of(scan_f, sib_f, after, p)
        gq_s[:, c] = (gq_l[:, c] + dot(scaled(g[:, c]), state, NT)).astype(BF16)

    arrived(sib_r.at[aligned(1 - core, half)], CR2)
    came_back(scan_r, BR, backward_at)
    for p in range(pairs):
        c = columns(p)
        state = state_of(scan_r, sib_r, 1.0 - after, p)
        gk_s[:, c] = (gk_l[:, c] + dot(v[:, c], state, NT)).astype(BF16)
        gv_s[:, c] = (gv_l[:, c] + dot(k[:, c], state)).astype(BF16)

    arrived(attn_r.at[:, pl.ds(0, (ys - 1) * width)], AT)

    sent(g.at[pl.ds(0, (ys - 1) * rows_y)], G)
    for which in (CF, CF2, CR, CR2):
        sent(own_f.at[pl.ds(0, half)], which)
    sent(attn_r.at[:, pl.ds(0, (ys - 1) * width)], AT)

    @pl.when(jnp.logical_not(owner))
    def _():
        sent(chip_f, OUT)
        sent(chip_r, OUT)

    @pl.when(owner)
    def _():
        sent(chip_f, OUT)
        sent(chip_r.at[pl.ds(0, half - chunk)], OUT)

    for places, which in ((forward_at, BF), (backward_at, BR)):

        @pl.when(among(z, places))
        def _(which=which):
            sent(line_out, which)
            sent(line_out.at[pl.ds(0, (zs - 1) * chunk)], which)
            for xx in range(xs):
                n = xx if which == BR else xs - 1 - xx
                if n:
                    pl.when(x == xx)(functools.partial(sent, totals.at[pl.ds(0, n * chunk)], TOT))


def write_out(*refs):
    copies = [pltpu.make_async_copy(refs[i], refs[4 + i], refs[8].at[i]) for i in range(4)]
    for copy in copies:
        copy.start()
    for copy in copies:
        copy.wait()


def shards(xs, zs, ys, forward_at, backward_at, back_order, query_rot, key_rot, value_rot, grad_out):
    tok, width = query_rot.shape
    half = width // PAIR * HALF
    chunk = half // len(forward_at)
    block = pltpu.VMEM((tok, width), BF16)
    wide = pltpu.VMEM((tok, width), F32)
    state = pltpu.VMEM((CORES * half, PAIR), F32)
    chip = pltpu.VMEM((half, PAIR), BF16)
    line = pltpu.VMEM((zs * chunk, PAIR), BF16)
    scan = pltpu.VMEM((CORES * half, PAIR), BF16)
    operands = [pltpu.with_memory_space_constraint(a, pltpu.HBM) for a in (query_rot, key_rot, value_rot, grad_out)]
    results = pl.pallas_call(
        functools.partial(kernel, xs, zs, ys, forward_at, backward_at, back_order),
        out_shape=(pltpu.VMEM(grad_out.shape, BF16), block, block, block),
        in_specs=[pl.BlockSpec(memory_space=pltpu.HBM)] * 4,
        out_specs=(pl.BlockSpec(memory_space=pltpu.VMEM),) * 4,
        scratch_shapes=[
            block, block, block, pltpu.VMEM(grad_out.shape, BF16), block,
            state, state, state, state,
            chip, chip,
            line, pltpu.VMEM((zs * chunk, PAIR), F32), line,
            pltpu.VMEM((xs * chunk, PAIR), F32),
            scan, scan,
            wide, wide, wide, wide,
            block,
            pltpu.SemaphoreType.DMA((4,)),
            pltpu.SemaphoreType.DMA((10,)),
            pltpu.SemaphoreType.DMA((10,)),
        ],
        compiler_params=pltpu.CompilerParams(
            collective_id=0, has_side_effects=True, vmem_limit_bytes=32 * 2**20
        ),
    )(*operands)
    return pl.pallas_call(
        write_out,
        out_shape=tuple(jax.ShapeDtypeStruct(a.shape, a.dtype) for a in results),
        in_specs=[pl.BlockSpec(memory_space=pltpu.VMEM)] * 4,
        out_specs=(pl.BlockSpec(memory_space=pltpu.HBM),) * 4,
        scratch_shapes=[pltpu.SemaphoreType.DMA((4,))],
    )(*[pltpu.with_memory_space_constraint(a, pltpu.VMEM) for a in results])


def solution(mesh, xs=XS, zs=ZS, forward_at=FORWARD_AT, backward_at=BACKWARD_AT, back_order=BACK_ORDER):
    in_specs = (P("seq", "head"), P("seq", "head"), P("seq", "head"), P(("seq", "head"), None))
    out_specs = (P(("seq", "head"), None), P("seq", "head"), P("seq", "head"), P("seq", "head"))
    return jax.shard_map(
        functools.partial(shards, xs, zs, mesh.shape["head"], forward_at, backward_at, back_order),
        mesh=mesh, in_specs=in_specs, out_specs=out_specs, check_vma=False,
    )
```
